1024 devices in a mesh: section: 16 (over z), expert: 64 (over x, y, core).
Axes of the slice: x: 4, y: 8, z: 16, core: 2. Of those that a mesh axis runs over, the one named last changes fastest.
Arguments:
- section_inputs: bfloat16 [16, 4096, 2560], P('section', 'expert'), may hold values from -6 to 6
- incoming: bfloat16 [1, 4096, 2560], P(None, 'expert'), may hold values from -6 to 6
- norm_gain: float32 [16, 2560], P('section'), may hold values from 0.5 to 1.5
- in_weights: bfloat16 [16, 40960, 1536], P('section', 'expert'), may hold values from -0.125 to 0.125
- down_weights: bfloat16 [16, 40960, 768], P('section', 'expert'), may hold values from -0.21875 to 0.21875
- expert_ids: int32 [2, 16, 4096, 2], P(None, 'section', 'expert'), may hold values from 0 to 15, all different within a row; in each aligned block of 64 rows (0 to 63, 64 to 127, ..., all dimensions but the last counted through in order) at most 10 rows name the same one
- route_weights: float32 [2, 16, 4096, 2], P(None, 'section', 'expert'), may hold values from 0.2 to 1
Outputs:
- final_state: bfloat16 [16, 4096, 2560], P('section', 'expert')
The draws below stay inside these ranges and needn't reach their ends.
Inputs may be any that keep to these rules, and one draw needn't show every extreme that they name: `expert_ids`: in each aligned block of 64 tokens (the tokens of one index of expert) of one step and section, no expert is named by more than 10 tokens; a token names 2 different experts.
All inputs are finite; a program needn't handle non-finite values.
Results may differ from the reference program's by a relative error of at most 0.019.
Values may be sent and summed in bfloat16 or wider, within the bound.
A program may use at most 32 MiB of HBM per device.

```python
import math
import jax
import jax.numpy as jnp
import numpy as np
from jax import lax

D = 2560
FF = 768
GROUP = 4
TOPK = 2
TICKS = 2
TOK_DEV = 64
EXPERTS = 16
CAP = 10
TOKENS = 4096
N_SECTION = 16


def block_levels(rng, dims, cuts, least, high):
    def one(dim, shards_of):
        steps = jax.random.uniform(jax.random.fold_in(jax.random.fold_in(rng, 6), dim), (shards_of,), jnp.float32, least / len(cuts), high / len(cuts))
        return jnp.repeat(jnp.exp(steps), dims[dim] // shards_of).reshape((-1,) + (1,) * (len(dims) - dim - 1))

    factor_of = one(*cuts[0])
    for cut in cuts[1:]:
        factor_of = factor_of * one(*cut)
    return factor_of


def routed_block(stream_key, own, number, rows, number_of, top, most, skew):
    order = jax.random.permutation(stream_key, number_of)
    crowded, common = load_shares(number_of, rows * top, most, skew, True), load_shares(number_of, rows * top, most, skew, False)
    places = jnp.arange(number_of)

    def named(sizes, turn):
        used = int((sizes > 0).sum())
        fixed = max(1, used // 4)
        passed = fixed + (places - fixed + turn * (used - fixed)) % max(1, number_of - fixed)
        return jnp.zeros((number_of,), jnp.int32).at[order[jnp.where(places < fixed, places, passed)]].set(jnp.asarray(sizes, jnp.int32))

    sizes = jnp.where(number % 4 == 0, named(crowded, number // 4), named(common, number - number // 4 - 1))
    mixed = jax.random.permutation(jax.random.fold_in(own, 3), number_of)
    source_of, taker = mixed[0:number_of // 2 * 2:2], mixed[1:number_of // 2 * 2:2]
    room = jnp.minimum(sizes[source_of] - 1, most - sizes[taker]) // 2
    room = jnp.where((source_of == order[0]) | (taker == order[0]) | (sizes[taker] == 0), 0, jnp.maximum(room, 0))
    passed = jax.random.randint(jax.random.fold_in(own, 4), (number_of // 2,), 0, 1 << 20) % (room + 1)
    sizes = sizes.at[source_of].add(-passed).at[taker].add(passed)
    labels = jnp.searchsorted(jnp.cumsum(sizes), jnp.arange(rows * top), side="right").astype(jnp.int32)
    table = labels.reshape(top, rows).T
    table = table[jax.random.permutation(jax.random.fold_in(own, 1), rows)]
    turn = jax.random.randint(jax.random.fold_in(own, 2), (rows, 1), 0, top)
    return jnp.take_along_axis(table, (jnp.arange(top)[None, :] + turn) % top, axis=1)


def load_shares(count, total, reach, lean, full):
    loads = [(1 << 20) // math.isqrt(rank ** lean) + 1 for rank in range(1, count + 1)]
    largest = reach if full else min(reach, max(-(-total // count), total * loads[0] // sum(loads)))
    least = 1 if total - largest >= count - 1 else 0
    counts, rest = [largest] + [least] * (count - 1), total - largest - least * (count - 1)
    while rest > 0:
        free = [i for i in range(1, count) if counts[i] < largest] or [i for i in range(1, count) if counts[i] < reach]
        whole, left = sum([loads[i] for i in free]), rest
        for i in free:
            extra = min(reach - counts[i], max(1, left * loads[i] // whole), rest)
            counts[i] = counts[i] + extra
            rest = rest - extra
    return np.array(counts)


def centred(key, extent, spread, bound, pieces=(), kind=jnp.bfloat16):
    loudness = block_levels(key, extent, pieces, -0.22, 0.18) if pieces else 1.0
    array = jax.random.normal(key, extent, jnp.float32) * spread * loudness
    return jnp.minimum(jnp.maximum(array, -bound), bound).astype(kind)


def setup_inputs(seed: int = 0) -> dict:
    streams_of = jax.random.split(jax.random.key(seed), 8)
    section_inputs = centred(streams_of[0], (N_SECTION, TOKENS, D), 1.0, 6.0, ((0, 16), (1, 64)))
    incoming = centred(streams_of[1], (TICKS - 1, TOKENS, D), 1.0, 6.0, ((1, 64),))
    norm_gain = jnp.clip(1.0 + 0.1 * jax.random.normal(streams_of[2], (N_SECTION, D), jnp.float32), 0.5, 1.5)
    in_weights = centred(streams_of[3], (N_SECTION, EXPERTS * D, 2 * FF), D ** -0.5, 0.125, ((0, 16), (1, 64)))
    down_weights = centred(streams_of[4], (N_SECTION, EXPERTS * D, FF), FF ** -0.5, 0.21875, ((0, 16), (1, 64)))
    expert_ids_keys = jax.random.split(jax.random.fold_in(streams_of[5], 1), TICKS * N_SECTION * TOKENS // TOK_DEV)
    expert_ids_turns = jax.random.permutation(jax.random.fold_in(streams_of[5], 3), TICKS * N_SECTION * TOKENS // TOK_DEV)
    expert_ids = jax.vmap(lambda own, number: routed_block(jax.random.fold_in(streams_of[5], 2), own, number, TOK_DEV, EXPERTS, TOPK, CAP, 2))(expert_ids_keys, expert_ids_turns).reshape((TICKS, N_SECTION, TOKENS, TOPK))
    route_weights = jnp.clip(0.2 + 0.8 * jax.random.uniform(streams_of[6], (TICKS, N_SECTION, TOKENS, TOPK), jnp.float32) ** block_levels(streams_of[6], (TICKS, N_SECTION, TOKENS, TOPK), ((1, 16), (2, 64)), -0.2, 0.2), 0.2, 1.0)
    return {"section_inputs": section_inputs, "incoming": incoming, "norm_gain": norm_gain, "in_weights": in_weights, "down_weights": down_weights, "expert_ids": expert_ids, "route_weights": route_weights}


def norm_rows(inputs, scale_row):
    widened = inputs.astype(jnp.float32)
    mean_square = lax.optimization_barrier(jnp.mean(widened * widened, axis=-1, keepdims=True))
    return (widened * lax.rsqrt(mean_square + 1e-06) * scale_row).astype(jnp.bfloat16)

def slot_tables(block_ids, block_weights):
    flat_ids = block_ids.reshape(-1)
    flat_weights = block_weights.reshape(-1)
    onehot = (flat_ids[:, None] == jnp.arange(EXPERTS, dtype=jnp.int32)[None, :]).astype(jnp.int32)
    before = jnp.cumsum(onehot, axis=0) - onehot
    slot_index = lax.optimization_barrier(jnp.sum(before * onehot, axis=1))
    slot_hot = (slot_index[:, None] == jnp.arange(CAP, dtype=jnp.int32)[None, :]).astype(jnp.float32)
    token_of = jnp.arange(TOK_DEV * TOPK, dtype=jnp.int32) // TOPK
    owner = (token_of[:, None] == jnp.arange(TOK_DEV, dtype=jnp.int32)[None, :]).astype(jnp.float32)
    expert_hot = onehot.astype(jnp.float32)
    picker = jnp.einsum('ae,ac,at->ect', expert_hot, slot_hot, owner)
    blender = jnp.einsum('ae,ac,at,a->tec', expert_hot, slot_hot, owner, flat_weights)
    return (picker, blender)

def expert_apply(token_rows, in_weight, down_weight, group_size):
    row_total = token_rows.shape[0]
    slice_width = D // group_size
    partials = jnp.einsum('rgd,gdh->grh', token_rows.reshape(row_total, group_size, slice_width).astype(jnp.float32), in_weight.reshape(group_size, slice_width, 2 * FF).astype(jnp.float32))
    rounded = lax.optimization_barrier(partials.astype(jnp.bfloat16))
    summed = lax.optimization_barrier(jnp.sum(rounded.astype(jnp.float32), axis=0))
    active = (jax.nn.silu(summed[:, :FF]) * summed[:, FF:]).astype(jnp.bfloat16)
    produced = lax.dot_general(active, down_weight, (((1,), (1,)), ((), ())), preferred_element_type=jnp.float32)
    return produced.astype(jnp.bfloat16)

def layer(inputs, scale_row, in_weights, down_weights, ids_now, weights_now):
    normed = norm_rows(inputs, scale_row)
    blocks = TOKENS // TOK_DEV
    picker, blender = jax.vmap(slot_tables)(ids_now.reshape(blocks, TOK_DEV, TOPK), weights_now.reshape(blocks, TOK_DEV, TOPK))
    dispatched = jnp.einsum('bect,btd->ebcd', picker, normed.reshape(blocks, TOK_DEV, D).astype(jnp.float32)).astype(jnp.bfloat16)

    def one_expert(operands):
        expert_rows, in_weight, down_weight = operands
        return expert_apply(expert_rows.reshape(blocks * CAP, D), in_weight, down_weight, GROUP)
    expert_outputs = lax.map(one_expert, (dispatched, in_weights.reshape(EXPERTS, D, 2 * FF), down_weights.reshape(EXPERTS, D, FF)))
    expert_outputs = expert_outputs.reshape(EXPERTS, blocks, CAP, D)
    mixture = jnp.einsum('btec,ebcd->btd', blender, expert_outputs.astype(jnp.float32))
    return (inputs.astype(jnp.float32) + mixture.reshape(TOKENS, D)).astype(jnp.bfloat16)

def reference(section_inputs, incoming, norm_gain, in_weights, down_weights, expert_ids, route_weights):

    def apply_section(operands):
        return layer(*operands)
    current = section_inputs
    for step_index in range(TICKS):
        current = lax.map(apply_section, (current, norm_gain, in_weights, down_weights, expert_ids[step_index], route_weights[step_index]))
        if step_index + 1 < TICKS:
            current = jnp.concatenate([incoming[step_index][None], current[:-1]], axis=0)
    return current
```

```python
import functools

import jax
import jax.numpy as jnp
from jax import lax
from jax.experimental import pallas as pl
from jax.experimental.pallas import tpu as pltpu
from jax.sharding import PartitionSpec as P

TICKS = 2
CAP = 10
NX = 4
MAIN = 16
REST = 4
BF16 = jnp.bfloat16
F32 = jnp.float32


def dot(a, b):
    return jnp.dot(a, b, preferred_element_type=F32)


def iota(shape, dim):
    return lax.broadcasted_iota(jnp.int32, shape, dim)


def slot_of(j, nx, ny):
    half = ny // 2
    experts = nx * half
    k = j - experts * MAIN
    rest_expert = ((k % (nx * REST)) // REST) * half + k // (nx * REST)
    is_main = j < experts * MAIN
    return jnp.where(is_main, j // MAIN, rest_expert), jnp.where(is_main, j % MAIN, MAIN + k % REST)


def kernel(
    dims,
    x_ref, inc_ref, gain_ref, win_hbm, wdn_hbm, ids_ref, rw_ref,
    out_ref,
    win, wdn, xs, wmeta, pm, bm, stat_s, stat_r, smain, srest, recv, yrest, xrest,
    part, core_in, kept, ysend, y_in, act, prod, back_x, back_y, ret, new, hand, fin,
    w_sem, swap_ss, swap_rs, meta_ss, meta_rs, stat_ss, stat_rs, main_ss, chunk_rs,
    yrest_ss, yrest_rs, xrest_ss, core_ss, core_rs, y_ss, y_rs, acty_ss, acty_rs,
    actc_ss, actc_rs, actf_ss, back_ss, backx_ss, backx_rs, backy_ss, back_rs,
    hand_ss, hand_rs, fin_ss, fin_rs,
):
    ns, nx, ny, tok, ds, ff, order, rest_at, fwd_slot = dims
    half = ny // 2
    experts = nx * half
    both = 2 * tok
    n_main = experts * MAIN
    n_rows = n_main + experts * REST
    n_chunk = half + 1
    main_rows = 2 * nx * MAIN
    rest_rows = nx * ny * REST
    yblk = nx * REST
    xblk = ny * REST
    width = 4 * ds

    s = lax.axis_index("section")
    me = lax.axis_index("expert")
    x = me // (2 * ny)
    y = (me // 2) % ny
    c = me % 2
    p = y % 2
    k = y // 2
    e = x * half + k

    def at(dx, to_y):
        return {"section": s, "expert": (((x + dx + nx) % nx) * ny + to_y) * 2 + c}

    far_x = sorted(range(nx), key=lambda dx: (-min(dx, nx - dx), dx))

    sibling = {"section": s, "expert": me + 1 - 2 * c}
    partner = {"section": s, "expert": (x * ny + y + 1 - 2 * p) * 2 + c}
    ahead = {"section": (s + 1) % ns, "expert": me}
    behind = {"section": (s + ns - 1) % ns, "expert": me}

    def send(src, dst, ss, rs, device):
        pltpu.make_async_remote_copy(
            src_ref=src, dst_ref=dst, send_sem=ss, recv_sem=rs, device_id=device,
            device_id_type=pl.DeviceIdType.MESH,
        ).start()

    def wait(ref, sem):
        pltpu.make_async_copy(ref, ref, sem).wait()

    def rows(start, count):
        return pl.ds(pl.multiple_of(start, count & -count), count)

    def columns(q, core):
        return pl.ds(pl.multiple_of(q * 2 * ds + core * ds, ds), ds)

    w_in = pltpu.make_async_copy(win_hbm.at[0], win, w_sem.at[0])
    w_down = pltpu.make_async_copy(wdn_hbm.at[0], wdn, w_sem.at[1])
    w_in.start()
    w_down.start()

    barrier = pltpu.get_barrier_semaphore()
    peers = [at(dx, (y + dy) % ny) for dy in range(ny) for dx in range(nx) if (dx, dy) != (0, 0)]
    peers += [sibling, ahead, behind]
    for device in peers:
        pl.semaphore_signal(barrier, inc=1, device_id=device, device_id_type=pl.DeviceIdType.MESH)

    own = rows(c * tok, tok)
    other = rows((1 - c) * tok, tok)
    lane = iota((tok, 128), 1)
    for t in range(TICKS):
        ids = ids_ref[t, 0]
        rw = rw_ref[t, 0]
        wmeta[t, own, :] = jnp.where(ids[:, 0:1] == lane, rw[:, 0:1], 0.0) + jnp.where(
            ids[:, 1:2] == lane, rw[:, 1:2], 0.0
        )
    for q in range(2):
        xs[0, q, own, :] = x_ref[0, :, columns(q, c)]
        xs[1, q, own, :] = inc_ref[0, :, columns(q, c)]
    pl.semaphore_wait(barrier, len(peers))

    for q in range(2):
        send(x_ref.at[0, :, columns(q, 1 - c)], xs.at[0, q, own, :], swap_ss.at[0, q], swap_rs.at[0, q], sibling)
    send(wmeta.at[:, own, :], wmeta.at[:, own, :], meta_ss, meta_rs, sibling)
    for q in range(2):
        send(inc_ref.at[0, :, columns(q, 1 - c)], xs.at[1, q, own, :], swap_ss.at[1, q], swap_rs.at[1, q], sibling)

    def earlier(shape, rank_dim):
        a, b = iota(shape, rank_dim), iota(shape, 1 - rank_dim)
        return ((b < a) & (b // tok == a // tok)).astype(BF16)

    def pick_table(t):
        w = jnp.transpose(wmeta[t])
        member = (w > 0).astype(BF16)
        number = dot(member, earlier((both, both), 1)) + (CAP * (iota((128, both), 1) // tok)).astype(F32)
        to_expert, to_number = slot_of(iota((n_rows, 128), 0), nx, ny)
        spread = (to_expert == iota((n_rows, 128), 1)).astype(BF16)
        _, to_number = slot_of(iota((n_rows, both), 0), nx, ny)
        hit = (dot(spread, member) > 0.5) & (dot(spread, number.astype(BF16)) == to_number.astype(F32))
        pm[t] = hit.astype(F32).astype(BF16)

    def blend_table(t):
        w = wmeta[t]
        member = (w > 0).astype(BF16)
        number = dot(earlier((both, both), 0), member) + (CAP * (iota((both, 128), 0) // tok)).astype(F32)
        to_expert, _ = slot_of(iota((128, n_rows), 1), nx, ny)
        spread = (to_expert == iota((128, n_rows), 0)).astype(BF16)
        _, to_number = slot_of(iota((both, n_rows), 1), nx, ny)
        hit = (dot(member, spread) > 0.5) & (dot(number.astype(BF16), spread) == to_number.astype(F32))
        bm[t] = jnp.where(hit, dot(w.astype(BF16), spread), 0.0).astype(BF16)

    def shuffle(out_dim):
        o = iota((rest_rows, rest_rows), out_dim)
        r = iota((rest_rows, rest_rows), 1 - out_dim)
        dx, source, j = o // xblk, (o % xblk) // REST, o % REST
        return (r == source * yblk + ((x - dx + nx) % nx) * REST + j).astype(F32).astype(BF16)

    def size(i):
        return rest_rows if i == rest_at else main_rows

    def pair_of(i):
        return order[i if i < rest_at else i - 1]

    parities = (p, 1 - p)

    def tick(t, carry):
        @pl.when(t == 0)
        def _():
            for q in range(2):
                wait(xs.at[0, q, other, :], swap_rs.at[0, q])

        square = jnp.zeros((both, 1), F32)
        for q in range(2):
            v = xs[t, q].astype(F32)
            square = square + jnp.sum(v * v, axis=-1, keepdims=True)
        stat_s[t] = jnp.broadcast_to(square, (both, 128))
        send(stat_s.at[t], stat_r.at[t], stat_ss.at[t], stat_rs.at[t], sibling)

        @pl.when(t == 0)
        def _():
            wait(wmeta.at[:, other, :], meta_rs)
            pick_table(0)

        wait(stat_r.at[t], stat_rs.at[t])
        scale = lax.rsqrt((square + stat_r[t, :, 0:1]) * (1.0 / width) + 1e-6)
        for q in range(2):
            normed = (xs[t, q].astype(F32) * scale * gain_ref[:, columns(q, c)]).astype(BF16)
            picked = dot(pm[t], normed).astype(BF16)
            smain[t, q * n_main : (q + 1) * n_main, :] = picked[:n_main]
            srest[t, q * half * yblk : (q + 1) * half * yblk, :] = picked[n_main:]

        for pairs in order:
            to_k = (k - pairs + half) % half
            dst = yrest.at[t, rows((2 * pairs + p) * yblk, yblk), :]
            for flip, to_p in enumerate(parities):
                src = srest.at[t, rows((to_p * half + to_k) * yblk, yblk), :]
                if pairs == 0 and flip == 0:
                    pltpu.make_async_copy(src, dst, yrest_rs.at[t]).start()
                else:
                    send(src, dst, yrest_ss.at[t], yrest_rs.at[t], at(0, 2 * to_k + to_p))
        for i in range(n_chunk):
            if i == rest_at:
                continue
            pairs = pair_of(i)
            to_k = (k - pairs + half) % half
            for flip, to_p in enumerate(parities):
                for dx in far_x:
                    to_x = (x - dx + nx) % nx
                    src = smain.at[t, rows(to_p * n_main + (to_x * half + to_k) * MAIN, MAIN), :]
                    dst = recv.at[t, i, rows((p * nx + dx) * MAIN, MAIN), :]
                    if pairs == 0 and flip == 0 and dx == 0:
                        pltpu.make_async_copy(src, dst, chunk_rs.at[t, i]).start()
                    else:
                        send(src, dst, main_ss.at[t], chunk_rs.at[t, i], at(-dx, 2 * to_k + to_p))

        @pl.when(t == 0)
        def _():
            blend_table(0)
            pick_table(1)
            blend_table(1)
            w_in.wait()
            w_down.wait()
            for q in range(2):
                wait(xs.at[1, q, other, :], swap_rs.at[1, q])

        def forward_rest():
            wait(yrest.at[t], yrest_rs.at[t])
            xrest[t] = dot(shuffle(0), yrest[t]).astype(BF16)
            for dx in range(nx):
                src = xrest.at[t, dx * xblk : (dx + 1) * xblk, :]
                dst = recv.at[t, rest_at, dx * xblk : (dx + 1) * xblk, :]
                if dx == 0:
                    pltpu.make_async_copy(src, dst, chunk_rs.at[t, rest_at]).start()
                else:
                    send(src, dst, xrest_ss.at[t], chunk_rs.at[t, rest_at], at(-dx, y))

        def stage_a(i):
            n = size(i)
            wait(recv.at[t, i, 0:n, :], chunk_rs.at[t, i])
            lhs = recv[t, i, 0:n, :]
            tile = ff // 2 if (ff // 2) % 128 == 0 else ff
            for j in range(0, 2 * ff, tile):
                part[t, i, 0:n, j : j + tile] = dot(lhs, win[:, j : j + tile]).astype(BF16)
            send(
                part.at[t, i, rows((1 - c) * (n // 2), n // 2), :], core_in.at[t, i, 0 : n // 2, :],
                core_ss.at[t, i], core_rs.at[t, i], sibling,
            )

        def stage_b(i):
            n = size(i)
            quarter = n // 4
            wait(core_in.at[t, i, 0 : n // 2, :], core_rs.at[t, i])

            def total(which):
                mine = part[t, i, rows(c * (n // 2) + which * quarter, quarter), :].astype(F32)
                return mine + core_in[t, i, rows(which * quarter, quarter), :].astype(F32)

            ysend[t, i, 0:quarter, :] = total(1 - p).astype(BF16)
            send(ysend.at[t, i, 0:quarter, :], y_in.at[t, i, 0:quarter, :], y_ss.at[t, i], y_rs.at[t, i], partner)
            kept[i, 0:quarter, :] = total(p)

        def stage_c(i):
            n = size(i)
            quarter = n // 4
            wait(y_in.at[t, i, 0:quarter, :], y_rs.at[t, i])
            pre = kept[i, 0:quarter, :] + y_in[t, i, 0:quarter, :].astype(F32)
            gate, up = pre[:, :ff], pre[:, ff:]
            mine = rows(c * (n // 2) + p * quarter, quarter)
            act[t, i, mine, :] = (gate / (1.0 + jnp.exp(-gate)) * up).astype(BF16)
            block = act.at[t, i, mine, :]
            send(block, block, acty_ss.at[t, i], acty_rs.at[t, i], partner)
            send(block, block, actc_ss.at[t, i], actc_rs.at[t, i], sibling)

        def stage_d(i):
            n = size(i)
            quarter = n // 4
            block = act.at[t, i, rows(c * (n // 2) + (1 - p) * quarter, quarter), :]
            wait(block, acty_rs.at[t, i])
            send(block, block, actf_ss.at[t, i], actc_rs.at[t, i], sibling)

        def stage_e(i):
            n = size(i)
            wait(act.at[t, i, rows((1 - c) * (n // 2), n // 2), :], actc_rs.at[t, i])
            prod[t, i, 0:n, :] = lax.dot_general(
                act[t, i, 0:n, :], wdn[...], (((1,), (1,)), ((), ())), preferred_element_type=F32
            ).astype(BF16)
            if i == rest_at:
                for dx in range(nx):
                    src = prod.at[t, i, dx * xblk : (dx + 1) * xblk, :]
                    dst = back_x.at[t, dx * xblk : (dx + 1) * xblk, :]
                    if dx == 0:
                        pltpu.make_async_copy(src, dst, backx_rs.at[t]).start()
                    else:
                        send(src, dst, backx_ss.at[t], backx_rs.at[t], at(dx, y))
                return
            dst = ret.at[t, p, rows(e * MAIN, MAIN), :]
            pairs = pair_of(i)
            to_k = (k + pairs) % half
            for flip, to_p in enumerate(parities):
                for dx in far_x:
                    src = prod.at[t, i, rows((to_p * nx + dx) * MAIN, MAIN), :]
                    if pairs == 0 and flip == 0 and dx == 0:
                        pltpu.make_async_copy(src, dst, back_rs.at[t]).start()
                    else:
                        send(src, dst, back_ss.at[t], back_rs.at[t], at(dx, 2 * to_k + to_p))

        def return_rest():
            wait(back_x.at[t], backx_rs.at[t])
            back_y[t] = dot(shuffle(1), back_x[t]).astype(BF16)
            dst = ret.at[t, p, rows(n_main + k * yblk, yblk), :]
            for pairs in order:
                to_k = (k + pairs) % half
                for flip, to_p in enumerate(parities):
                    src = back_y.at[t, rows((2 * pairs + to_p) * yblk, yblk), :]
                    if pairs == 0 and flip == 0:
                        pltpu.make_async_copy(src, dst, back_rs.at[t]).start()
                    else:
                        send(src, dst, backy_ss.at[t], back_rs.at[t], at(0, 2 * to_k + to_p))

        for n in range(n_chunk + 5):
            if n == rest_at + 5:
                return_rest()
            for lag, stage in ((4, stage_e), (3, stage_d), (2, stage_c), (1, stage_b)):
                if 0 <= n - lag < n_chunk:
                    stage(n - lag)
            if n == fwd_slot:
                forward_rest()
            if n < n_chunk:
                stage_a(n)

        wait(ret.at[t], back_rs.at[t])
        for q in range(2):
            mixed = dot(bm[t], ret[t, q])
            new[t, q] = (xs[t, q].astype(F32) + mixed).astype(BF16)

            @pl.when(t == 0)
            def _():
                send(new.at[0, q], hand.at[q], hand_ss.at[q], hand_rs.at[q], ahead)

            @pl.when(t == 1)
            def _():
                send(new.at[1, q, other, :], fin.at[q], fin_ss.at[q], fin_rs.at[q], sibling)

        @pl.when(t == 0)
        def _():
            for q in range(2):
                wait(hand.at[q], hand_rs.at[q])
                xs[1, q] = jnp.where(s == 0, xs[1, q], hand[q])

        return carry

    lax.fori_loop(0, TICKS, tick, 0)

    for q in range(2):
        out_ref[0, :, columns(q, c)] = new[1, q, own, :]
    for q in range(2):
        wait(fin.at[q], fin_rs.at[q])
        out_ref[0, :, columns(q, 1 - c)] = fin[q]

    for q in range(2):
        wait(xs.at[0, q, own, :], swap_ss.at[0, q])
        wait(xs.at[1, q, own, :], swap_ss.at[1, q])
        wait(hand.at[q], hand_ss.at[q])
        wait(fin.at[q], fin_ss.at[q])
    wait(wmeta.at[:, own, :], meta_ss)

    def drain(t, carry):
        wait(stat_s.at[t], stat_ss.at[t])
        wait(smain.at[t, 0 : (nx * ny - 1) * MAIN, :], main_ss.at[t])
        wait(srest.at[t, 0 : (ny - 1) * yblk, :], yrest_ss.at[t])
        wait(xrest.at[t, 0 : (nx - 1) * xblk, :], xrest_ss.at[t])
        for i in range(n_chunk):
            n = size(i)
            quarter = act.at[t, i, 0 : n // 4, :]
            wait(core_in.at[t, i, 0 : n // 2, :], core_ss.at[t, i])
            wait(ysend.at[t, i, 0 : n // 4, :], y_ss.at[t, i])
            wait(quarter, acty_ss.at[t, i])
            wait(quarter, actc_ss.at[t, i])
            wait(quarter, actf_ss.at[t, i])
        wait(smain.at[t, 0 : (nx * ny - 1) * MAIN, :], back_ss.at[t])
        wait(back_x.at[t, 0 : (nx - 1) * xblk, :], backx_ss.at[t])
        wait(back_y.at[t, 0 : (ny - 1) * yblk, :], backy_ss.at[t])
        return carry

    lax.fori_loop(0, TICKS, drain, 0)


def body(section_inputs, incoming, norm_gain, in_weights, down_weights, expert_ids, route_weights):
    ns, count = lax.axis_size("section"), lax.axis_size("expert")
    nx = NX
    ny = count // (2 * nx)
    half = ny // 2
    experts = nx * half
    tok = section_inputs.shape[1]
    ds, ff = in_weights.shape[1], down_weights.shape[2]
    order = sorted(range(half), key=lambda d: (-min(d, half - d), d))
    n_chunk = half + 1
    rest_at, fwd_slot = 2, 1
    dims = (ns, nx, ny, tok, ds, ff, order, rest_at, fwd_slot)
    both = 2 * tok
    n_main, n_rest = experts * MAIN, experts * REST
    n_rows = n_main + n_rest
    most = max(2 * nx * MAIN, nx * ny * REST)
    rest_rows = nx * ny * REST

    def vmem(*shape, dtype=BF16):
        return pltpu.VMEM(shape, dtype)

    def dma(*shape):
        return pltpu.SemaphoreType.DMA(shape) if shape else pltpu.SemaphoreType.DMA

    n = n_chunk
    scratch = [
        vmem(ds, 2 * ff), vmem(ds, ff), vmem(2, 2, both, ds), vmem(2, both, 128, dtype=F32),
        vmem(2, n_rows, both), vmem(2, both, n_rows),
        vmem(2, both, 128, dtype=F32), vmem(2, both, 128, dtype=F32),
        vmem(2, 2 * n_main, ds), vmem(2, 2 * n_rest, ds), vmem(2, n, most, ds),
        vmem(2, rest_rows, ds), vmem(2, rest_rows, ds),
        vmem(2, n, most, 2 * ff), vmem(2, n, most // 2, 2 * ff), vmem(n, most // 4, 2 * ff, dtype=F32),
        vmem(2, n, most // 4, 2 * ff), vmem(2, n, most // 4, 2 * ff), vmem(2, n, most, ff), vmem(2, n, most, ds),
        vmem(2, rest_rows, ds), vmem(2, rest_rows, ds), vmem(2, 2, n_rows, ds),
        vmem(2, 2, both, ds), vmem(2, both, ds), vmem(2, tok, ds),
        dma(2), dma(2, 2), dma(2, 2), dma(), dma(), dma(2), dma(2), dma(2), dma(2, n),
        dma(2), dma(2), dma(2), dma(2, n), dma(2, n), dma(2, n), dma(2, n), dma(2, n), dma(2, n),
        dma(2, n), dma(2, n), dma(2, n), dma(2), dma(2), dma(2), dma(2), dma(2),
        dma(2), dma(2), dma(2), dma(2),
    ]
    in_vmem = pl.BlockSpec(memory_space=pltpu.VMEM)
    anywhere = pl.BlockSpec(memory_space=pl.ANY)
    slots = 2 * 2 * n_rows
    return pl.pallas_call(
        functools.partial(kernel, dims),
        out_shape=jax.ShapeDtypeStruct(section_inputs.shape, section_inputs.dtype),
        in_specs=[in_vmem, in_vmem, in_vmem, anywhere, anywhere, in_vmem, in_vmem],
        out_specs=in_vmem,
        scratch_shapes=scratch,
        compiler_params=pltpu.CompilerParams(
            collective_id=0, has_side_effects=True, vmem_limit_bytes=48 * 1024 * 1024
        ),
        cost_estimate=pl.CostEstimate(
            flops=2 * slots * ds * 3 * ff, bytes_accessed=2 * ds * 3 * ff, transcendentals=slots * ff
        ),
        name="relay",
    )(section_inputs, incoming, norm_gain, in_weights, down_weights, expert_ids, route_weights)


def solution(mesh):
    placed = (
        P("section", "expert", None),
        P(None, "expert", None),
        P("section", None),
        P("section", "expert", None),
        P("section", "expert", None),
        P(None, "section", "expert", None),
        P(None, "section", "expert", None),
    )
    return jax.shard_map(
        body, mesh=mesh, in_specs=placed, out_specs=P("section", "expert", None), check_vma=False
    )
```

```python
import functools

import jax
import jax.numpy as jnp
from jax import lax
from jax.experimental import pallas as pl
from jax.experimental.pallas import tpu as pltpu
from jax.sharding import PartitionSpec as P

TICKS = 2
CAP = 10
NX = 4
MAIN = 16
REST = 4
BF16 = jnp.bfloat16
F32 = jnp.float32


def dot(a, b):
    return jnp.dot(a, b, preferred_element_type=F32)


def iota(shape, dim):
    return lax.broadcasted_iota(jnp.int32, shape, dim)


def kernel(
    dims,
    x_hbm, inc_hbm, gain_hbm, win_hbm, wdn_hbm, ids_ref, rw_ref,
    out_ref,
    state, inc, gain, win, wdn, wmeta, pm, bm, normed, smain, srest, recv, yrest, xrest,
    part, y_in, act, prod, back_x, back_y, ret, mix_s, mix_r, new, hand,
    load, w_ss, w_rs, meta_ss, meta_rs, norm_ss, norm_rs, main_ss, chunk_rs,
    yrest_ss, yrest_rs, xrest_ss, y_ss, y_rs, acty_ss, acty_rs,
    back_ss, backx_ss, backx_rs, backy_ss, back_rs, mix_ss, mix_rs, hand_ss, hand_rs,
):
    ns, nx, ny, tok, ds, ff, groups, chunks, fwd_slot = dims
    half = ny // 2
    nm, nh = nx // 2, half // 2
    both = 2 * tok
    wide = 2 * ds
    n_main = nm * half * MAIN
    yblk = nx * REST
    xblk = half * REST
    n_rest = nh * yblk
    n_rows = n_main + n_rest
    group_rows = 2 * nm * MAIN
    rest_rows = nx * xblk
    width = 4 * ds

    s = lax.axis_index("section")
    me = lax.axis_index("expert")
    x = me // (2 * ny)
    y = (me // 2) % ny
    c = me % 2
    p = y % 2
    k = y // 2
    parities = (p, 1 - p)

    def at(dx, to_y):
        return {"section": s, "expert": (((x + dx + nx) % nx) * ny + to_y) * 2 + c}

    sibling = {"section": s, "expert": me + 1 - 2 * c}
    partner = {"section": s, "expert": (x * ny + y + 1 - 2 * p) * 2 + c}
    ahead = {"section": (s + 1) % ns, "expert": me}
    behind = {"section": (s + ns - 1) % ns, "expert": me}

    def send(src, dst, ss, rs, device):
        pltpu.make_async_remote_copy(
            src_ref=src, dst_ref=dst, send_sem=ss, recv_sem=rs, device_id=device,
            device_id_type=pl.DeviceIdType.MESH,
        ).start()

    def copy(src, dst, sem):
        pltpu.make_async_copy(src, dst, sem).start()

    def wait(ref, sem):
        pltpu.make_async_copy(ref, ref, sem).wait()

    def rows(start, count):
        return pl.ds(pl.multiple_of(start, count & -count), count)

    own = rows(c * tok, tok)
    other = rows((1 - c) * tok, tok)
    slice_own = rows(c * ds, ds)
    slice_other = rows((1 - c) * ds, ds)

    copy(x_hbm.at[0], state.at[0], load.at[0])
    copy(gain_hbm, gain, load.at[1])
    copy(win_hbm.at[0], win.at[slice_own, :], load.at[2])
    copy(wdn_hbm.at[0], wdn.at[slice_own, :], load.at[3])
    copy(inc_hbm.at[0], inc, load.at[4])

    barrier = pltpu.get_barrier_semaphore()
    peers = [at(dx, (y + dy) % ny) for dy in range(ny) for dx in range(nx) if (dx, dy) != (0, 0)]
    peers += [sibling, ahead, behind]
    for device in peers:
        pl.semaphore_signal(barrier, inc=1, device_id=device, device_id_type=pl.DeviceIdType.MESH)

    lane = iota((128, tok), 0)
    for t in range(TICKS):
        ids = ids_ref[t, 0]
        rw = rw_ref[t, 0]
        w = jnp.where(ids[0:1] == lane, rw[0:1], 0.0) + jnp.where(ids[1:2] == lane, rw[1:2], 0.0)
        if tok < 128:
            w = jnp.concatenate([w, jnp.zeros((128, 128 - tok), F32)], axis=1)
        wmeta[t, own, :] = jnp.transpose(w)[:tok]

    def normalise(t):
        v = state[t].astype(F32)
        scale = lax.rsqrt(jnp.sum(v * v, axis=-1, keepdims=True) * (1.0 / width) + 1e-6)
        normed[t, own, :] = (v * scale * gain[...]).astype(BF16)

    wait(state.at[0], load.at[0])
    wait(gain, load.at[1])
    normalise(0)
    pl.semaphore_wait(barrier, len(peers))
    send(wmeta.at[:, own, :], wmeta.at[:, own, :], meta_ss, meta_rs, sibling)

    def earlier(shape, rank_dim):
        a, b = iota(shape, rank_dim), iota(shape, 1 - rank_dim)
        return ((b < a) & (b // tok == a // tok)).astype(BF16)

    def slot_of(j):
        m = j // (half * MAIN)
        main_expert = ((x - c - 2 * m + 2 * nx) % nx) * half + (j // MAIN) % half
        i = j - n_main
        rest_expert = ((i % yblk) // REST) * half + (k - c - 2 * (i // yblk) + 2 * half) % half
        is_main = j < n_main
        return jnp.where(is_main, main_expert, rest_expert), jnp.where(is_main, j % MAIN, MAIN + i % REST)

    def pick_table(t):
        w = jnp.transpose(wmeta[t])
        member = (w > 0).astype(BF16)
        number = dot(member, earlier((both, both), 1)) + (CAP * (iota((128, both), 1) // tok)).astype(F32)
        to_expert, _ = slot_of(iota((n_rows, 128), 0))
        spread = (to_expert == iota((n_rows, 128), 1)).astype(BF16)
        _, to_number = slot_of(iota((n_rows, both), 0))
        hit = (dot(spread, member) > 0.5) & (dot(spread, number.astype(BF16)) == to_number.astype(F32))
        pm[t] = hit.astype(F32).astype(BF16)

    def blend_table(t):
        w = wmeta[t]
        member = (w > 0).astype(BF16)
        number = dot(earlier((both, both), 0), member) + (CAP * (iota((both, 128), 0) // tok)).astype(F32)
        to_expert, _ = slot_of(iota((128, n_rows), 1))
        spread = (to_expert == iota((128, n_rows), 0)).astype(BF16)
        _, to_number = slot_of(iota((both, n_rows), 1))
        hit = (dot(member, spread) > 0.5) & (dot(number.astype(BF16), spread) == to_number.astype(F32))
        bm[t] = jnp.where(hit, dot(w.astype(BF16), spread), 0.0).astype(BF16)

    def shuffle(out_dim):
        o = iota((rest_rows, rest_rows), out_dim)
        r = iota((rest_rows, rest_rows), 1 - out_dim)
        dx, source, j = o // xblk, (o % xblk) // REST, o % REST
        return (r == source * yblk + ((x - dx + nx) % nx) * REST + j).astype(F32).astype(BF16)

    start, chunk_of, first, size, row = {}, {}, [], [], 0
    for i, count in enumerate(chunks):
        first.append(row)
        for g in groups[len(start) : len(start) + count]:
            start[g], chunk_of[g] = row, i
            row += rest_rows if g is None else group_rows
        size.append(row - first[i])
    members = [[g for g in groups if chunk_of[g] == i] for i in range(len(chunks))]

    def blocks(i):
        return [(g, flip, m) for m in range(nm)[::-1] for flip in range(2) for g in members[i] if g is not None]

    def self_or_send(is_self, src, dst, ss, rs, device):
        if not is_self:
            send(src, dst, ss, rs, device)
            return

        @pl.when(c == 0)
        def _():
            copy(src, dst, rs)

        @pl.when(c == 1)
        def _():
            send(src, dst, ss, rs, device)

    def tick(t, carry):
        send(normed.at[t, own, :], normed.at[t, own, :], norm_ss.at[t], norm_rs.at[t], sibling)

        @pl.when(t == 0)
        def _():
            wait(win.at[slice_own, :], load.at[2])
            send(win.at[slice_own, :], win.at[slice_own, :], w_ss.at[0], w_rs.at[0], sibling)
            wait(wdn.at[slice_own, :], load.at[3])
            send(wdn.at[slice_own, :], wdn.at[slice_own, :], w_ss.at[1], w_rs.at[1], sibling)
            wait(wmeta.at[:, other, :], meta_rs)
            pick_table(0)

        wait(normed.at[t, other, :], norm_rs.at[t])
        for q in range(2):
            all_rows = normed[t, :, q * wide : (q + 1) * wide]
            srest[t, q] = dot(pm[t, n_main:, :], all_rows).astype(BF16)
        for h in range(nh):
            to_k = (k - c - 2 * h + 2 * half) % half
            for flip, to_p in enumerate(parities):
                self_or_send(
                    h == 0 and flip == 0,
                    srest.at[t, to_p, h * yblk : (h + 1) * yblk, :], yrest.at[t, rows((2 * h + p) * yblk, yblk), :],
                    yrest_ss.at[t], yrest_rs.at[t], at(0, 2 * to_k + to_p),
                )
        for q in range(2):
            all_rows = normed[t, :, q * wide : (q + 1) * wide]
            smain[t, q] = dot(pm[t, :n_main, :], all_rows).astype(BF16)
        for i in range(len(chunks)):
            for pairs, flip, m in blocks(i):
                to_k, to_p = (k - pairs + half) % half, parities[flip]
                self_or_send(
                    pairs == 0 and flip == 0 and m == 0,
                    smain.at[t, to_p, rows((m * half + to_k) * MAIN, MAIN), :],
                    recv.at[t, rows(start[pairs] + (p * nm + m) * MAIN, MAIN), :],
                    main_ss.at[t], chunk_rs.at[t, i], at(-c - 2 * m + nx, 2 * to_k + to_p),
                )

        @pl.when(t == 0)
        def _():
            blend_table(0)
            pick_table(1)
            blend_table(1)
            wait(inc, load.at[4])
            wait(win.at[slice_other, :], w_rs.at[0])
            wait(wdn.at[slice_other, :], w_rs.at[1])

        def forward_rest():
            wait(yrest.at[t], yrest_rs.at[t])
            xrest[t] = dot(shuffle(0), yrest[t]).astype(BF16)
            for dx in range(nx)[::-1]:
                src = xrest.at[t, dx * xblk : (dx + 1) * xblk, :]
                dst = recv.at[t, start[None] + dx * xblk : start[None] + (dx + 1) * xblk, :]
                if dx == 0:
                    copy(src, dst, chunk_rs.at[t, chunk_of[None]])
                else:
                    send(src, dst, xrest_ss.at[t], chunk_rs.at[t, chunk_of[None]], at(-dx, y))

        def stage_a(i):
            a, n = first[i], size[i]
            wait(recv.at[t, a : a + n, :], chunk_rs.at[t, i])
            lhs = recv[t, a : a + n, :]
            tile = ff // 2 if (ff // 2) % 128 == 0 else ff
            for j in range(0, 2 * ff, tile):
                part[t, a : a + n, j : j + tile] = dot(lhs, win[:, j : j + tile]).astype(BF16)
            send(
                part.at[t, rows(a + (1 - p) * (n // 2), n // 2), :], y_in.at[t, a // 2 : (a + n) // 2, :],
                y_ss.at[t, i], y_rs.at[t, i], partner,
            )

        def stage_c(i):
            a, n = first[i], size[i]
            wait(y_in.at[t, a // 2 : (a + n) // 2, :], y_rs.at[t, i])
            mine = rows(a + p * (n // 2), n // 2)
            pre = part[t, mine, :].astype(F32) + y_in[t, a // 2 : (a + n) // 2, :].astype(F32)
            gate, up = pre[:, :ff], pre[:, ff:]
            act[t, mine, :] = (gate / (1.0 + jnp.exp(-gate)) * up).astype(BF16)
            send(act.at[t, mine, :], act.at[t, mine, :], acty_ss.at[t, i], acty_rs.at[t, i], partner)

        def stage_e(i):
            a, n = first[i], size[i]
            wait(act.at[t, rows(a + (1 - p) * (n // 2), n // 2), :], acty_rs.at[t, i])
            prod[t, a : a + n, :] = lax.dot_general(
                act[t, a : a + n, :], wdn[...], (((1,), (1,)), ((), ())), preferred_element_type=F32
            ).astype(BF16)
            if chunk_of[None] == i:
                for dx in range(nx)[::-1]:
                    src = prod.at[t, start[None] + dx * xblk : start[None] + (dx + 1) * xblk, :]
                    dst = back_x.at[t, dx * xblk : (dx + 1) * xblk, :]
                    if dx == 0:
                        copy(src, dst, backx_rs.at[t])
                    else:
                        send(src, dst, backx_ss.at[t], backx_rs.at[t], at(dx, y))
            for pairs, flip, m in blocks(i):
                to_k, to_p = (k + pairs) % half, parities[flip]
                self_or_send(
                    pairs == 0 and flip == 0 and m == 0,
                    prod.at[t, rows(start[pairs] + (to_p * nm + m) * MAIN, MAIN), :],
                    ret.at[t, p, rows((m * half + k) * MAIN, MAIN), :],
                    back_ss.at[t], back_rs.at[t], at(c + 2 * m, 2 * to_k + to_p),
                )

        def return_rest():
            wait(back_x.at[t], backx_rs.at[t])
            back_y[t] = dot(shuffle(1), back_x[t]).astype(BF16)
            for h in range(nh):
                to_k = (k + c + 2 * h) % half
                for flip, to_p in enumerate(parities):
                    self_or_send(
                        h == 0 and flip == 0,
                        back_y.at[t, rows((2 * h + to_p) * yblk, yblk), :],
                        ret.at[t, p, n_main + h * yblk : n_main + (h + 1) * yblk, :],
                        backy_ss.at[t], back_rs.at[t], at(0, 2 * to_k + to_p),
                    )

        n_chunk = len(chunks)
        for n in range(n_chunk + 3):
            if n == fwd_slot:
                forward_rest()
            if n == chunk_of[None] + 3:
                return_rest()
            if 0 <= n - 2 < n_chunk:
                stage_e(n - 2)
            if 0 <= n - 1 < n_chunk:
                stage_c(n - 1)
            if n < n_chunk:
                stage_a(n)

        wait(ret.at[t], back_rs.at[t])
        for q in range(2):
            mix_s[t, q] = dot(bm[t, other, :], ret[t, q]).astype(BF16)
            send(mix_s.at[t, q], mix_r.at[t, q], mix_ss.at[t, q], mix_rs.at[t, q], sibling)
        for q in range(2):
            mixed = state[t, :, q * wide : (q + 1) * wide].astype(F32) + dot(bm[t, own, :], ret[t, q])
            wait(mix_r.at[t, q], mix_rs.at[t, q])
            new[t, q] = (mixed + mix_r[t, q].astype(F32)).astype(BF16)

            @pl.when(t == 0)
            def _():
                send(new.at[0, q], hand.at[q], hand_ss.at[q], hand_rs.at[q], ahead)

        @pl.when(t == 0)
        def _():
            for q in range(2):
                wait(hand.at[q], hand_rs.at[q])
                part_of = slice(q * wide, (q + 1) * wide)
                state[1, :, part_of] = jnp.where(s == 0, inc[:, part_of], hand[q])
            normalise(1)

        return carry

    lax.fori_loop(0, TICKS, tick, 0)
    for q in range(2):
        out_ref[0, :, q * wide : (q + 1) * wide] = new[1, q]

    for q in range(2):
        wait(hand.at[q], hand_ss.at[q])
    wait(wmeta.at[:, own, :], meta_ss)
    wait(win.at[slice_own, :], w_ss.at[0])
    wait(wdn.at[slice_own, :], w_ss.at[1])

    def drain(t, carry):
        def sent(ref, block, count, sem):
            @pl.when(c == 0)
            def _():
                wait(ref.at[t, 0 : block * count, :], sem.at[t])

            @pl.when(c == 1)
            def _():
                wait(ref.at[t, 0 : block * (count + 1), :], sem.at[t])

        wait(normed.at[t, own, :], norm_ss.at[t])
        sent(recv, MAIN, 2 * nm * half - 1, main_ss)
        sent(yrest, yblk, 2 * nh - 1, yrest_ss)
        wait(xrest.at[t, 0 : (nx - 1) * xblk, :], xrest_ss.at[t])
        for i in range(len(chunks)):
            a, n = first[i], size[i]
            wait(y_in.at[t, a // 2 : (a + n) // 2, :], y_ss.at[t, i])
            wait(act.at[t, a // 2 : (a + n) // 2, :], acty_ss.at[t, i])
        sent(recv, MAIN, 2 * nm * half - 1, back_ss)
        wait(back_x.at[t, 0 : (nx - 1) * xblk, :], backx_ss.at[t])
        sent(yrest, yblk, 2 * nh - 1, backy_ss)
        for q in range(2):
            wait(mix_s.at[t, q], mix_ss.at[t, q])
        return carry

    lax.fori_loop(0, TICKS, drain, 0)


def body(section_inputs, incoming, norm_gain, in_weights, down_weights, expert_ids, route_weights):
    ns, count = lax.axis_size("section"), lax.axis_size("expert")
    nx = NX
    ny = count // (2 * nx)
    half = ny // 2
    tok = section_inputs.shape[1]
    ds, ff = in_weights.shape[1], down_weights.shape[2]
    groups = [None] + sorted(range(half), key=lambda d: (-min(d, half - d), d))
    chunks = [2, 3] if half == 4 else [2, 1]
    fwd_slot = 0
    dims = (ns, nx, ny, tok, ds, ff, groups, chunks, fwd_slot)
    both, wide = 2 * tok, 2 * ds
    nm, nh = nx // 2, half // 2
    n_main, n_rest = nm * half * MAIN, nh * nx * REST
    n_rows = n_main + n_rest
    rest_rows = nx * half * REST
    work = half * 2 * nm * MAIN + rest_rows

    def vmem(*shape, dtype=BF16):
        return pltpu.VMEM(shape, dtype)

    def dma(*shape):
        return pltpu.SemaphoreType.DMA(shape) if shape else pltpu.SemaphoreType.DMA

    n = len(chunks)
    scratch = [
        vmem(2, tok, 2 * wide), vmem(tok, 2 * wide), vmem(1, 2 * wide, dtype=F32),
        vmem(wide, 2 * ff), vmem(wide, ff), vmem(2, both, 128, dtype=F32),
        vmem(2, n_rows, both), vmem(2, both, n_rows), vmem(2, both, 2 * wide),
        vmem(2, 2, n_main, wide), vmem(2, 2, n_rest, wide), vmem(2, work, wide),
        vmem(2, rest_rows, wide), vmem(2, rest_rows, wide),
        vmem(2, work, 2 * ff), vmem(2, work // 2, 2 * ff), vmem(2, work, ff), vmem(2, work, wide),
        vmem(2, rest_rows, wide), vmem(2, rest_rows, wide), vmem(2, 2, n_rows, wide),
        vmem(2, 2, tok, wide), vmem(2, 2, tok, wide), vmem(2, 2, tok, wide), vmem(2, tok, wide),
        dma(5), dma(2), dma(2), dma(), dma(), dma(2), dma(2), dma(2), dma(2, n),
        dma(2), dma(2), dma(2), dma(2, n), dma(2, n), dma(2, n), dma(2, n),
        dma(2), dma(2), dma(2), dma(2), dma(2), dma(2, 2), dma(2, 2), dma(2), dma(2),
    ]
    in_vmem = pl.BlockSpec(memory_space=pltpu.VMEM)
    anywhere = pl.BlockSpec(memory_space=pl.ANY)
    return pl.pallas_call(
        functools.partial(kernel, dims),
        out_shape=jax.ShapeDtypeStruct(section_inputs.shape, section_inputs.dtype),
        in_specs=[anywhere] * 5 + [in_vmem] * 2,
        out_specs=in_vmem,
        scratch_shapes=scratch,
        compiler_params=pltpu.CompilerParams(
            collective_id=0, has_side_effects=True, vmem_limit_bytes=60 * 1024 * 1024
        ),
        cost_estimate=pl.CostEstimate(
            flops=2 * 2 * work * wide * 3 * ff, bytes_accessed=2 * ds * 3 * ff, transcendentals=work * ff
        ),
        name="relay",
    )(
        section_inputs, incoming, norm_gain, in_weights, down_weights,
        jnp.swapaxes(expert_ids, 2, 3), jnp.swapaxes(route_weights, 2, 3),
    )


def solution(mesh):
    placed = (
        P("section", "expert", None),
        P(None, "expert", None),
        P("section", None),
        P("section", "expert", None),
        P("section", "expert", None),
        P(None, "section", "expert", None),
        P(None, "section", "expert", None),
    )
    return jax.shard_map(
        body, mesh=mesh, in_specs=placed, out_specs=P("section", "expert", None), check_vma=False
    )
```

```python
import functools

import jax
import jax.numpy as jnp
from jax import lax
from jax.experimental import pallas as pl
from jax.experimental.pallas import tpu as pltpu
from jax.sharding import PartitionSpec as P

TICKS = 2
CAP = 10
NX = 4
MAIN = 16
REST = 4
BF16 = jnp.bfloat16
F32 = jnp.float32


def dot(a, b):
    return jnp.dot(a, b, preferred_element_type=F32)


def iota(shape, dim):
    return lax.broadcasted_iota(jnp.int32, shape, dim)


def kernel(
    dims,
    x_hbm, inc_hbm, gain_hbm, win_hbm, wdn_hbm, ids_ref, rw_ref,
    out_ref,
    state, inc, gain, win, wdn, wmeta, pm, bm, normed, smain, srest, recv, yrest, xrest,
    part, y_in, act, prod, back_x, back_y, ret, mix_s, mix_r, new, hand,
    load, w_ss, w_rs, meta_ss, meta_rs, norm_ss, norm_rs, main_ss, chunk_rs,
    yrest_ss, yrest_rs, xrest_ss, y_ss, y_rs, acty_ss, acty_rs,
    back_ss, backx_ss, backx_rs, backy_ss, back_rs, mix_ss, mix_rs, hand_ss, hand_rs,
):
    ns, nx, ny, tok, ds, ff, groups, chunks, fwd_slot, cuts, piece = dims
    half = ny // 2
    nm, nh = nx // 2, half // 2
    both = 2 * tok
    wide = 2 * ds
    n_main = nm * half * MAIN
    yblk = nx * REST
    xblk = half * REST
    n_rest = nh * yblk
    n_rows = n_main + n_rest
    parts = list(enumerate(slice(a, b) for a, b in zip([0] + cuts, cuts)))
    group_rows = 2 * nm * MAIN
    rest_rows = nx * xblk
    width = 4 * ds

    s = lax.axis_index("section")
    me = lax.axis_index("expert")
    x = me // (2 * ny)
    y = (me // 2) % ny
    c = me % 2
    p = y % 2
    k = y // 2
    parities = (p, 1 - p)

    def at(dx, to_y):
        return {"section": s, "expert": (((x + dx + nx) % nx) * ny + to_y) * 2 + c}

    sibling = {"section": s, "expert": me + 1 - 2 * c}
    partner = {"section": s, "expert": (x * ny + y + 1 - 2 * p) * 2 + c}
    ahead = {"section": (s + 1) % ns, "expert": me}
    behind = {"section": (s + ns - 1) % ns, "expert": me}

    def send(src, dst, ss, rs, device):
        pltpu.make_async_remote_copy(
            src_ref=src, dst_ref=dst, send_sem=ss, recv_sem=rs, device_id=device,
            device_id_type=pl.DeviceIdType.MESH,
        ).start()

    def copy(src, dst, sem):
        pltpu.make_async_copy(src, dst, sem).start()

    def wait(ref, sem):
        pltpu.make_async_copy(ref, ref, sem).wait()

    def rows(start, count):
        return pl.ds(pl.multiple_of(start, count & -count), count)

    own = rows(c * tok, tok)
    other = rows((1 - c) * tok, tok)
    slice_own = rows(c * ds, ds)
    slice_other = rows((1 - c) * ds, ds)

    copy(x_hbm.at[0], state.at[0], load.at[0])
    copy(gain_hbm, gain, load.at[1])
    copy(win_hbm.at[0], win.at[slice_own, :], load.at[2])
    copy(wdn_hbm.at[0], wdn.at[slice_own, :], load.at[3])
    copy(inc_hbm.at[0], inc, load.at[4])

    barrier = pltpu.get_barrier_semaphore()
    peers = [at(dx, (y + dy) % ny) for dy in range(ny) for dx in range(nx) if (dx, dy) != (0, 0)]
    peers += [sibling, ahead, behind]
    for device in peers:
        pl.semaphore_signal(barrier, inc=1, device_id=device, device_id_type=pl.DeviceIdType.MESH)

    lane = iota((128, tok), 0)
    for t in range(TICKS):
        ids = ids_ref[t, 0]
        rw = rw_ref[t, 0]
        w = jnp.where(ids[0:1] == lane, rw[0:1], 0.0) + jnp.where(ids[1:2] == lane, rw[1:2], 0.0)
        if tok < 128:
            w = jnp.concatenate([w, jnp.zeros((128, 128 - tok), F32)], axis=1)
        wmeta[t, own, :] = jnp.transpose(w)[:tok]

    def normalise(t):
        v = state[t].astype(F32)
        scale = lax.rsqrt(jnp.sum(v * v, axis=-1, keepdims=True) * (1.0 / width) + 1e-6)
        normed[t, own, :] = (v * scale * gain[...]).astype(BF16)

    wait(state.at[0], load.at[0])
    wait(gain, load.at[1])
    normalise(0)
    pl.semaphore_wait(barrier, len(peers))
    send(wmeta.at[:, own, :], wmeta.at[:, own, :], meta_ss, meta_rs, sibling)

    def earlier(shape, rank_dim):
        a, b = iota(shape, rank_dim), iota(shape, 1 - rank_dim)
        return ((b < a) & (b // tok == a // tok)).astype(BF16)

    def slot_of(j):
        m = j // (half * MAIN)
        main_expert = ((x - c - 2 * m + 2 * nx) % nx) * half + (j // MAIN) % half
        i = j - n_main
        rest_expert = ((i % yblk) // REST) * half + (k - c - 2 * (i // yblk) + 2 * half) % half
        is_main = j < n_main
        return jnp.where(is_main, main_expert, rest_expert), jnp.where(is_main, j % MAIN, MAIN + i % REST)

    def pick_table(t):
        w = jnp.transpose(wmeta[t])
        member = (w > 0).astype(BF16)
        number = dot(member, earlier((both, both), 1)) + (CAP * (iota((128, both), 1) // tok)).astype(F32)
        to_expert, _ = slot_of(iota((n_rows, 128), 0))
        spread = (to_expert == iota((n_rows, 128), 1)).astype(BF16)
        _, to_number = slot_of(iota((n_rows, both), 0))
        hit = (dot(spread, member) > 0.5) & (dot(spread, number.astype(BF16)) == to_number.astype(F32))
        pm[t] = hit.astype(F32).astype(BF16)

    def blend_table(t):
        w = wmeta[t]
        member = (w > 0).astype(BF16)
        number = dot(earlier((both, both), 0), member) + (CAP * (iota((both, 128), 0) // tok)).astype(F32)
        to_expert, _ = slot_of(iota((128, n_rows), 1))
        spread = (to_expert == iota((128, n_rows), 0)).astype(BF16)
        _, to_number = slot_of(iota((both, n_rows), 1))
        hit = (dot(member, spread) > 0.5) & (dot(number.astype(BF16), spread) == to_number.astype(F32))
        bm[t] = jnp.where(hit, dot(w.astype(BF16), spread), 0.0).astype(BF16)

    def shuffle(out_dim):
        o = iota((rest_rows, rest_rows), out_dim)
        r = iota((rest_rows, rest_rows), 1 - out_dim)
        dx, source, j = o // xblk, (o % xblk) // REST, o % REST
        return (r == source * yblk + ((x - dx + nx) % nx) * REST + j).astype(F32).astype(BF16)

    start, chunk_of, first, size, row = {}, {}, [], [], 0
    for i, count in enumerate(chunks):
        first.append(row)
        for g in groups[len(start) : len(start) + count]:
            start[g], chunk_of[g] = row, i
            row += rest_rows if g is None else group_rows
        size.append(row - first[i])
    members = [[g for g in groups if chunk_of[g] == i] for i in range(len(chunks))]

    def blocks(i):
        return [(g, flip, m) for m in range(nm)[::-1] for flip in range(2) for g in members[i] if g is not None]

    def pieces(i):
        b = min(piece, size[i] // 2)
        return [(v // b, v, b) for v in range(0, size[i] // 2, b)]

    def self_or_send(is_self, src, dst, ss, rs, device):
        if not is_self:
            send(src, dst, ss, rs, device)
            return

        @pl.when(c == 0)
        def _():
            copy(src, dst, rs)

        @pl.when(c == 1)
        def _():
            send(src, dst, ss, rs, device)

    def tick(t, carry):
        send(normed.at[t, own, :], normed.at[t, own, :], norm_ss.at[t], norm_rs.at[t], sibling)

        @pl.when(t == 0)
        def _():
            wait(win.at[slice_own, :], load.at[2])
            send(win.at[slice_own, :], win.at[slice_own, :], w_ss.at[0], w_rs.at[0], sibling)
            wait(wdn.at[slice_own, :], load.at[3])
            send(wdn.at[slice_own, :], wdn.at[slice_own, :], w_ss.at[1], w_rs.at[1], sibling)
            wait(wmeta.at[:, other, :], meta_rs)
            pick_table(0)

        wait(normed.at[t, other, :], norm_rs.at[t])
        for q in range(2):
            all_rows = normed[t, :, q * wide : (q + 1) * wide]
            srest[t, q] = dot(pm[t, n_main:, :], all_rows).astype(BF16)
        for h in range(nh):
            to_k = (k - c - 2 * h + 2 * half) % half
            for flip, to_p in enumerate(parities):
                self_or_send(
                    h == 0 and flip == 0,
                    srest.at[t, to_p, h * yblk : (h + 1) * yblk, :], yrest.at[t, rows((2 * h + p) * yblk, yblk), :],
                    yrest_ss.at[t], yrest_rs.at[t], at(0, 2 * to_k + to_p),
                )
        for q in range(2):
            all_rows = normed[t, :, q * wide : (q + 1) * wide]
            smain[t, q] = dot(pm[t, :n_main, :], all_rows).astype(BF16)
        for i in range(len(chunks)):
            for pairs, flip, m in blocks(i):
                to_k, to_p = (k - pairs + half) % half, parities[flip]
                self_or_send(
                    pairs == 0 and flip == 0 and m == 0,
                    smain.at[t, to_p, rows((m * half + to_k) * MAIN, MAIN), :],
                    recv.at[t, rows(start[pairs] + (p * nm + m) * MAIN, MAIN), :],
                    main_ss.at[t], chunk_rs.at[t, i], at(-c - 2 * m + nx, 2 * to_k + to_p),
                )

        @pl.when(t == 0)
        def _():
            blend_table(0)
            pick_table(1)
            blend_table(1)
            wait(inc, load.at[4])
            wait(win.at[slice_other, :], w_rs.at[0])
            wait(wdn.at[slice_other, :], w_rs.at[1])

        def forward_rest():
            wait(yrest.at[t], yrest_rs.at[t])
            xrest[t] = dot(shuffle(0), yrest[t]).astype(BF16)
            for dx in range(nx)[::-1]:
                src = xrest.at[t, dx * xblk : (dx + 1) * xblk, :]
                dst = recv.at[t, start[None] + dx * xblk : start[None] + (dx + 1) * xblk, :]
                if dx == 0:
                    copy(src, dst, chunk_rs.at[t, chunk_of[None]])
                else:
                    send(src, dst, xrest_ss.at[t], chunk_rs.at[t, chunk_of[None]], at(-dx, y))

        def stage_a(i):
            a, n = first[i], size[i]
            wait(recv.at[t, a : a + n, :], chunk_rs.at[t, i])
            lhs = recv[t, a : a + n, :]
            tile = ff // 2 if (ff // 2) % 128 == 0 else ff
            for j in range(0, 2 * ff, tile):
                part[t, a : a + n, j : j + tile] = dot(lhs, win[:, j : j + tile]).astype(BF16)
            for u, v, b in pieces(i):
                send(
                    part.at[t, rows(a + (1 - p) * (n // 2) + v, b), :], y_in.at[t, a // 2 + v : a // 2 + v + b, :],
                    y_ss.at[t, i], y_rs.at[t, i, u], partner,
                )

        def stage_c(i):
            a, n = first[i], size[i]
            for u, v, b in pieces(i):
                wait(y_in.at[t, a // 2 + v : a // 2 + v + b, :], y_rs.at[t, i, u])
                mine = rows(a + p * (n // 2) + v, b)
                pre = part[t, mine, :].astype(F32) + y_in[t, a // 2 + v : a // 2 + v + b, :].astype(F32)
                gate, up = pre[:, :ff], pre[:, ff:]
                act[t, mine, :] = (gate / (1.0 + jnp.exp(-gate)) * up).astype(BF16)
                send(act.at[t, mine, :], act.at[t, mine, :], acty_ss.at[t, i], acty_rs.at[t, i], partner)

        def stage_e(i):
            a, n = first[i], size[i]
            wait(act.at[t, rows(a + (1 - p) * (n // 2), n // 2), :], acty_rs.at[t, i])
            lhs = act[t, a : a + n, :]
            for h, cols in parts:
                prod[t, a : a + n, cols] = lax.dot_general(
                    lhs, wdn[cols, :], (((1,), (1,)), ((), ())), preferred_element_type=F32
                ).astype(BF16)
                if chunk_of[None] == i:
                    for dx in range(nx)[::-1]:
                        src = prod.at[t, start[None] + dx * xblk : start[None] + (dx + 1) * xblk, cols]
                        dst = back_x.at[t, dx * xblk : (dx + 1) * xblk, cols]
                        if dx == 0:
                            copy(src, dst, backx_rs.at[t, h])
                        else:
                            send(src, dst, backx_ss.at[t, h], backx_rs.at[t, h], at(dx, y))
                for pairs, flip, m in blocks(i):
                    to_k, to_p = (k + pairs) % half, parities[flip]
                    self_or_send(
                        pairs == 0 and flip == 0 and m == 0,
                        prod.at[t, rows(start[pairs] + (to_p * nm + m) * MAIN, MAIN), cols],
                        ret.at[t, p, rows((m * half + k) * MAIN, MAIN), cols],
                        back_ss.at[t], back_rs.at[t, h], at(c + 2 * m, 2 * to_k + to_p),
                    )

        def return_rest():
            for g, cols in parts:
                wait(back_x.at[t, :, cols], backx_rs.at[t, g])
                back_y[t, :, cols] = dot(shuffle(1), back_x[t, :, cols]).astype(BF16)
                for h in range(nh):
                    to_k = (k + c + 2 * h) % half
                    for flip, to_p in enumerate(parities):
                        self_or_send(
                            h == 0 and flip == 0,
                            back_y.at[t, rows((2 * h + to_p) * yblk, yblk), cols],
                            ret.at[t, p, n_main + h * yblk : n_main + (h + 1) * yblk, cols],
                            backy_ss.at[t], back_rs.at[t, g], at(0, 2 * to_k + to_p),
                        )

        n_chunk = len(chunks)
        for n in range(n_chunk + 3):
            if n == fwd_slot:
                forward_rest()
            if n == chunk_of[None] + 3:
                return_rest()
            if 0 <= n - 1 < n_chunk:
                stage_c(n - 1)
            if 0 <= n - 2 < n_chunk:
                stage_e(n - 2)
            if n < n_chunk:
                stage_a(n)

        for h, cols in parts:
            wait(ret.at[t, :, :, cols], back_rs.at[t, h])
            for q in range(2):
                mix_s[t, q, :, cols] = dot(bm[t, other, :], ret[t, q, :, cols]).astype(BF16)
            send(mix_s.at[t, :, :, cols], mix_r.at[t, :, :, cols], mix_ss.at[t, h], mix_rs.at[t, h], sibling)
            mixed = [
                state[t, :, q * wide + cols.start : q * wide + cols.stop].astype(F32)
                + dot(bm[t, own, :], ret[t, q, :, cols])
                for q in range(2)
            ]
            wait(mix_r.at[t, :, :, cols], mix_rs.at[t, h])
            for q in range(2):
                new[t, q, :, cols] = (mixed[q] + mix_r[t, q, :, cols].astype(F32)).astype(BF16)

            @pl.when(t == 0)
            def _():
                send(new.at[0, :, :, cols], hand.at[:, :, cols], hand_ss.at[h], hand_rs.at[h], ahead)

        @pl.when(t == 0)
        def _():
            for h, cols in parts:
                wait(hand.at[:, :, cols], hand_rs.at[h])
                for q in range(2):
                    part_of = slice(q * wide + cols.start, q * wide + cols.stop)
                    state[1, :, part_of] = jnp.where(s == 0, inc[:, part_of], hand[q, :, cols])
            normalise(1)

        return carry

    lax.fori_loop(0, TICKS, tick, 0)
    for q in range(2):
        out_ref[0, :, q * wide : (q + 1) * wide] = new[1, q]

    for h, cols in parts:
        wait(hand.at[:, :, cols], hand_ss.at[h])
    wait(wmeta.at[:, own, :], meta_ss)
    wait(win.at[slice_own, :], w_ss.at[0])
    wait(wdn.at[slice_own, :], w_ss.at[1])

    def drain(t, carry):
        def sent(ref, block, count, sem):
            @pl.when(c == 0)
            def _():
                wait(ref.at[t, 0 : block * count, :], sem.at[t])

            @pl.when(c == 1)
            def _():
                wait(ref.at[t, 0 : block * (count + 1), :], sem.at[t])

        wait(normed.at[t, own, :], norm_ss.at[t])
        sent(recv, MAIN, 2 * nm * half - 1, main_ss)
        sent(yrest, yblk, 2 * nh - 1, yrest_ss)
        wait(xrest.at[t, 0 : (nx - 1) * xblk, :], xrest_ss.at[t])
        for i in range(len(chunks)):
            a, n = first[i], size[i]
            wait(y_in.at[t, a // 2 : (a + n) // 2, :], y_ss.at[t, i])
            wait(act.at[t, a // 2 : (a + n) // 2, :], acty_ss.at[t, i])
        sent(recv, MAIN, 2 * nm * half - 1, back_ss)
        for h, cols in parts:
            wait(back_x.at[t, 0 : (nx - 1) * xblk, cols], backx_ss.at[t, h])
            wait(mix_s.at[t, :, :, cols], mix_ss.at[t, h])
        sent(yrest, yblk, 2 * nh - 1, backy_ss)
        return carry

    lax.fori_loop(0, TICKS, drain, 0)


def body(section_inputs, incoming, norm_gain, in_weights, down_weights, expert_ids, route_weights):
    ns, count = lax.axis_size("section"), lax.axis_size("expert")
    nx = NX
    ny = count // (2 * nx)
    half = ny // 2
    tok = section_inputs.shape[1]
    ds, ff = in_weights.shape[1], down_weights.shape[2]
    groups = [None] + sorted(range(half), key=lambda d: (-min(d, half - d), d))
    chunks = [2, 3] if half == 4 else [2, 1]
    fwd_slot = 0
    cuts = [ds * 4 // 5, ds * 8 // 5, 2 * ds]
    piece = 32
    dims = (ns, nx, ny, tok, ds, ff, groups, chunks, fwd_slot, cuts, piece)
    both, wide = 2 * tok, 2 * ds
    nm, nh = nx // 2, half // 2
    n_main, n_rest = nm * half * MAIN, nh * nx * REST
    n_rows = n_main + n_rest
    rest_rows = nx * half * REST
    work = half * 2 * nm * MAIN + rest_rows

    def vmem(*shape, dtype=BF16):
        return pltpu.VMEM(shape, dtype)

    def dma(*shape):
        return pltpu.SemaphoreType.DMA(shape) if shape else pltpu.SemaphoreType.DMA

    n, h = len(chunks), len(cuts)
    scratch = [
        vmem(2, tok, 2 * wide), vmem(tok, 2 * wide), vmem(1, 2 * wide, dtype=F32),
        vmem(wide, 2 * ff), vmem(wide, ff), vmem(2, both, 128, dtype=F32),
        vmem(2, n_rows, both), vmem(2, both, n_rows), vmem(2, both, 2 * wide),
        vmem(2, 2, n_main, wide), vmem(2, 2, n_rest, wide), vmem(2, work, wide),
        vmem(2, rest_rows, wide), vmem(2, rest_rows, wide),
        vmem(2, work, 2 * ff), vmem(2, work // 2, 2 * ff), vmem(2, work, ff), vmem(2, work, wide),
        vmem(2, rest_rows, wide), vmem(2, rest_rows, wide), vmem(2, 2, n_rows, wide),
        vmem(2, 2, tok, wide), vmem(2, 2, tok, wide), vmem(2, 2, tok, wide), vmem(2, tok, wide),
        dma(5), dma(2), dma(2), dma(), dma(), dma(2), dma(2), dma(2), dma(2, n),
        dma(2), dma(2), dma(2), dma(2, n), dma(2, n, work // piece), dma(2, n), dma(2, n),
        dma(2), dma(2, h), dma(2, h), dma(2), dma(2, h), dma(2, h), dma(2, h), dma(h), dma(h),
    ]
    in_vmem = pl.BlockSpec(memory_space=pltpu.VMEM)
    anywhere = pl.BlockSpec(memory_space=pl.ANY)
    return pl.pallas_call(
        functools.partial(kernel, dims),
        out_shape=jax.ShapeDtypeStruct(section_inputs.shape, section_inputs.dtype),
        in_specs=[anywhere] * 5 + [in_vmem] * 2,
        out_specs=in_vmem,
        scratch_shapes=scratch,
        compiler_params=pltpu.CompilerParams(
            collective_id=0, has_side_effects=True, vmem_limit_bytes=60 * 1024 * 1024
        ),
        cost_estimate=pl.CostEstimate(
            flops=2 * 2 * work * wide * 3 * ff, bytes_accessed=2 * ds * 3 * ff, transcendentals=work * ff
        ),
        name="relay",
    )(
        section_inputs, incoming, norm_gain, in_weights, down_weights,
        jnp.swapaxes(expert_ids, 2, 3), jnp.swapaxes(route_weights, 2, 3),
    )


def solution(mesh):
    placed = (
        P("section", "expert", None),
        P(None, "expert", None),
        P("section", None),
        P("section", "expert", None),
        P("section", "expert", None),
        P(None, "section", "expert", None),
        P(None, "section", "expert", None),
    )
    return jax.shard_map(
        body, mesh=mesh, in_specs=placed, out_specs=P("section", "expert", None), check_vma=False
    )
```

```python
import functools

import jax
import jax.numpy as jnp
from jax import lax
from jax.experimental import pallas as pl
from jax.experimental.pallas import tpu as pltpu
from jax.sharding import PartitionSpec as P

TICKS = 2
CAP = 10
NX = 4
MAIN = 16
REST = 4
BF16 = jnp.bfloat16
F32 = jnp.float32


def dot(a, b):
    return jnp.dot(a, b, preferred_element_type=F32)


def iota(shape, dim):
    return lax.broadcasted_iota(jnp.int32, shape, dim)


def kernel(
    dims,
    x_hbm, inc_hbm, gain_hbm, win_hbm, wdn_hbm, ids_ref, rw_ref,
    out_ref,
    state, inc, gain, win, wdn, wmeta, pm, bm, normed, smain, srest, recv, yrest, xrest,
    part, y_in, act, prod, back_x, back_y, ret, mix_s, mix_r, new, hand,
    load, w_ss, w_rs, meta_ss, meta_rs, norm_ss, norm_rs, main_ss, chunk_rs,
    yrest_ss, yrest_rs, xrest_ss, y_ss, y_rs, acty_ss, acty_rs,
    back_ss, backx_ss, backx_rs, backy_ss, back_rs, mix_ss, mix_rs, hand_ss, hand_rs,
):
    ns, nx, ny, tok, ds, ff, groups, chunks, fwd_slot, cuts, piece = dims
    half = ny // 2
    nm, nh = nx // 2, half // 2
    both = 2 * tok
    wide = 2 * ds
    n_main = nm * half * MAIN
    yblk = nx * REST
    xblk = half * REST
    n_rest = nh * yblk
    n_rows = n_main + n_rest
    parts = list(enumerate(slice(a, b) for a, b in zip([0] + cuts, cuts)))
    group_rows = 2 * nm * MAIN
    rest_rows = nx * xblk
    width = 4 * ds

    s = lax.axis_index("section")
    me = lax.axis_index("expert")
    x = me // (2 * ny)
    y = (me // 2) % ny
    c = me % 2
    p = y % 2
    k = y // 2
    parities = (p, 1 - p)

    def at(dx, to_y):
        return {"section": s, "expert": (((x + dx + nx) % nx) * ny + to_y) * 2 + c}

    sibling = {"section": s, "expert": me + 1 - 2 * c}
    partner = {"section": s, "expert": (x * ny + y + 1 - 2 * p) * 2 + c}
    ahead = {"section": (s + 1) % ns, "expert": me}
    behind = {"section": (s + ns - 1) % ns, "expert": me}

    def send(src, dst, ss, rs, device):
        pltpu.make_async_remote_copy(
            src_ref=src, dst_ref=dst, send_sem=ss, recv_sem=rs, device_id=device,
            device_id_type=pl.DeviceIdType.MESH,
        ).start()

    def copy(src, dst, sem):
        pltpu.make_async_copy(src, dst, sem).start()

    def wait(ref, sem):
        pltpu.make_async_copy(ref, ref, sem).wait()

    def rows(start, count):
        return pl.ds(pl.multiple_of(start, count & -count), count)

    own = rows(c * tok, tok)
    other = rows((1 - c) * tok, tok)
    slice_own = rows(c * ds, ds)
    slice_other = rows((1 - c) * ds, ds)

    copy(x_hbm.at[0], state.at[0], load.at[0])
    copy(gain_hbm, gain, load.at[1])
    copy(win_hbm.at[0], win.at[slice_own, :], load.at[2])
    copy(wdn_hbm.at[0], wdn.at[slice_own, :], load.at[3])
    copy(inc_hbm.at[0], inc, load.at[4])

    barrier = pltpu.get_barrier_semaphore()
    peers = [at(dx, (y + dy) % ny) for dy in range(ny) for dx in range(nx) if (dx, dy) != (0, 0)]
    peers += [sibling, ahead, behind]
    for device in peers:
        pl.semaphore_signal(barrier, inc=1, device_id=device, device_id_type=pl.DeviceIdType.MESH)

    lane = iota((128, tok), 0)
    for t in range(TICKS):
        ids = ids_ref[t, 0]
        rw = rw_ref[t, 0]
        w = jnp.where(ids[0:1] == lane, rw[0:1], 0.0) + jnp.where(ids[1:2] == lane, rw[1:2], 0.0)
        if tok < 128:
            w = jnp.concatenate([w, jnp.zeros((128, 128 - tok), F32)], axis=1)
        wmeta[t, own, :] = jnp.transpose(w)[:tok]

    def normalise(t):
        v = state[t].astype(F32)
        scale = lax.rsqrt(jnp.sum(v * v, axis=-1, keepdims=True) * (1.0 / width) + 1e-6)
        normed[t, own, :] = (v * scale * gain[...]).astype(BF16)

    wait(state.at[0], load.at[0])
    wait(gain, load.at[1])
    normalise(0)
    pl.semaphore_wait(barrier, len(peers))
    send(wmeta.at[:, own, :], wmeta.at[:, own, :], meta_ss, meta_rs, sibling)

    def earlier(shape, rank_dim):
        a, b = iota(shape, rank_dim), iota(shape, 1 - rank_dim)
        return ((b < a) & (b // tok == a // tok)).astype(BF16)

    def slot_of(j):
        m = j // (half * MAIN)
        main_expert = ((x - c - 2 * m + 2 * nx) % nx) * half + (j // MAIN) % half
        i = j - n_main
        rest_expert = ((i % yblk) // REST) * half + (k - c - 2 * (i // yblk) + 2 * half) % half
        is_main = j < n_main
        return jnp.where(is_main, main_expert, rest_expert), jnp.where(is_main, j % MAIN, MAIN + i % REST)

    def pick_table(t):
        w = jnp.transpose(wmeta[t])
        member = (w > 0).astype(BF16)
        number = dot(member, earlier((both, both), 1)) + (CAP * (iota((128, both), 1) // tok)).astype(F32)
        to_expert, _ = slot_of(iota((n_rows, 128), 0))
        spread = (to_expert == iota((n_rows, 128), 1)).astype(BF16)
        _, to_number = slot_of(iota((n_rows, both), 0))
        hit = (dot(spread, member) > 0.5) & (dot(spread, number.astype(BF16)) == to_number.astype(F32))
        pm[t] = hit.astype(F32).astype(BF16)

    def blend_table(t):
        w = wmeta[t]
        member = (w > 0).astype(BF16)
        number = dot(earlier((both, both), 0), member) + (CAP * (iota((both, 128), 0) // tok)).astype(F32)
        to_expert, _ = slot_of(iota((128, n_rows), 1))
        spread = (to_expert == iota((128, n_rows), 0)).astype(BF16)
        _, to_number = slot_of(iota((both, n_rows), 1))
        hit = (dot(member, spread) > 0.5) & (dot(number.astype(BF16), spread) == to_number.astype(F32))
        bm[t] = jnp.where(hit, dot(w.astype(BF16), spread), 0.0).astype(BF16)

    def shuffle(out_dim):
        o = iota((rest_rows, rest_rows), out_dim)
        r = iota((rest_rows, rest_rows), 1 - out_dim)
        dx, source, j = o // xblk, (o % xblk) // REST, o % REST
        return (r == source * yblk + ((x - dx + nx) % nx) * REST + j).astype(F32).astype(BF16)

    start, chunk_of, first, size, row = {}, {}, [], [], 0
    for i, count in enumerate(chunks):
        first.append(row)
        for g in groups[len(start) : len(start) + count]:
            start[g], chunk_of[g] = row, i
            row += rest_rows if g is None else group_rows
        size.append(row - first[i])
    members = [[g for g in groups if chunk_of[g] == i] for i in range(len(chunks))]

    def blocks(i):
        return [(g, flip, m) for m in range(nm)[::-1] for flip in range(2) for g in members[i] if g is not None]

    def pieces(i):
        b = min(piece, size[i] // 2)
        return [(v // b, v, b) for v in range(0, size[i] // 2, b)]

    def self_or_send(is_self, src, dst, ss, rs, device):
        if not is_self:
            send(src, dst, ss, rs, device)
            return

        @pl.when(c == 0)
        def _():
            copy(src, dst, rs)

        @pl.when(c == 1)
        def _():
            send(src, dst, ss, rs, device)

    def tick(t, carry):
        send(normed.at[t, own, :], normed.at[t, own, :], norm_ss.at[t], norm_rs.at[t], sibling)

        @pl.when(t == 0)
        def _():
            wait(win.at[slice_own, :], load.at[2])
            send(win.at[slice_own, :], win.at[slice_own, :], w_ss.at[0], w_rs.at[0], sibling)
            wait(wdn.at[slice_own, :], load.at[3])
            send(wdn.at[slice_own, :], wdn.at[slice_own, :], w_ss.at[1], w_rs.at[1], sibling)
            wait(wmeta.at[:, other, :], meta_rs)
            pick_table(0)

        wait(normed.at[t, other, :], norm_rs.at[t])
        for q in range(2):
            all_rows = normed[t, :, q * wide : (q + 1) * wide]
            srest[t, q] = dot(pm[t, n_main:, :], all_rows).astype(BF16)
        for h in range(nh):
            to_k = (k - c - 2 * h + 2 * half) % half
            for flip, to_p in enumerate(parities):
                self_or_send(
                    h == 0 and flip == 0,
                    srest.at[t, to_p, h * yblk : (h + 1) * yblk, :], yrest.at[t, rows((2 * h + p) * yblk, yblk), :],
                    yrest_ss.at[t], yrest_rs.at[t], at(0, 2 * to_k + to_p),
                )
        for q in range(2):
            all_rows = normed[t, :, q * wide : (q + 1) * wide]
            smain[t, q] = dot(pm[t, :n_main, :], all_rows).astype(BF16)
        for i in range(len(chunks)):
            for pairs, flip, m in blocks(i):
                to_k, to_p = (k - pairs + half) % half, parities[flip]
                self_or_send(
                    pairs == 0 and flip == 0 and m == 0,
                    smain.at[t, to_p, rows((m * half + to_k) * MAIN, MAIN), :],
                    recv.at[t, rows(start[pairs] + (p * nm + m) * MAIN, MAIN), :],
                    main_ss.at[t], chunk_rs.at[t, i], at(-c - 2 * m + nx, 2 * to_k + to_p),
                )

        @pl.when(t == 0)
        def _():
            blend_table(0)
            pick_table(1)
            blend_table(1)
            wait(inc, load.at[4])
            wait(win.at[slice_other, :], w_rs.at[0])
            wait(wdn.at[slice_other, :], w_rs.at[1])

        def forward_rest():
            wait(yrest.at[t], yrest_rs.at[t])
            xrest[t] = dot(shuffle(0), yrest[t]).astype(BF16)
            for dx in range(nx)[::-1]:
                src = xrest.at[t, dx * xblk : (dx + 1) * xblk, :]
                dst = recv.at[t, start[None] + dx * xblk : start[None] + (dx + 1) * xblk, :]
                if dx == 0:
                    copy(src, dst, chunk_rs.at[t, chunk_of[None]])
                else:
                    send(src, dst, xrest_ss.at[t], chunk_rs.at[t, chunk_of[None]], at(-dx, y))

        def stage_a(i):
            a, n = first[i], size[i]
            wait(recv.at[t, a : a + n, :], chunk_rs.at[t, i])
            lhs = recv[t, a : a + n, :]
            tile = ff // 2 if (ff // 2) % 128 == 0 else ff
            for j in range(0, 2 * ff, tile):
                part[t, a : a + n, j : j + tile] = dot(lhs, win[:, j : j + tile]).astype(BF16)
            for u, v, b in pieces(i):
                send(
                    part.at[t, rows(a + (1 - p) * (n // 2) + v, b), :], y_in.at[t, a // 2 + v : a // 2 + v + b, :],
                    y_ss.at[t, i], y_rs.at[t, i, u], partner,
                )

        def stage_c(i):
            a, n = first[i], size[i]
            for u, v, b in pieces(i):
                wait(y_in.at[t, a // 2 + v : a // 2 + v + b, :], y_rs.at[t, i, u])
                mine = rows(a + p * (n // 2) + v, b)
                pre = part[t, mine, :].astype(F32) + y_in[t, a // 2 + v : a // 2 + v + b, :].astype(F32)
                gate, up = pre[:, :ff], pre[:, ff:]
                act[t, mine, :] = (gate / (1.0 + jnp.exp(-gate)) * up).astype(BF16)
                send(act.at[t, mine, :], act.at[t, mine, :], acty_ss.at[t, i], acty_rs.at[t, i], partner)

        def down(a, n, cols):
            prod[t, a : a + n, cols] = lax.dot_general(
                act[t, a : a + n, :], wdn[cols, :], (((1,), (1,)), ((), ())), preferred_element_type=F32
            ).astype(BF16)

        def arrived(i):
            a, n = first[i], size[i]
            wait(act.at[t, rows(a + (1 - p) * (n // 2), n // 2), :], acty_rs.at[t, i])

        def send_rest():
            arrived(chunk_of[None])
            for h, cols in parts:
                down(start[None], rest_rows, cols)
                for dx in range(nx)[::-1]:
                    src = prod.at[t, start[None] + dx * xblk : start[None] + (dx + 1) * xblk, cols]
                    dst = back_x.at[t, dx * xblk : (dx + 1) * xblk, cols]
                    if dx == 0:
                        copy(src, dst, backx_rs.at[t, h])
                    else:
                        send(src, dst, backx_ss.at[t, h], backx_rs.at[t, h], at(dx, y))

        def stage_e(i):
            a, n = first[i], size[i]
            if chunk_of[None] == i:
                a, n = a + rest_rows, n - rest_rows
            else:
                arrived(i)
            for h, cols in parts:
                down(a, n, cols)
                for pairs, flip, m in blocks(i):
                    to_k, to_p = (k + pairs) % half, parities[flip]
                    self_or_send(
                        pairs == 0 and flip == 0 and m == 0,
                        prod.at[t, rows(start[pairs] + (to_p * nm + m) * MAIN, MAIN), cols],
                        ret.at[t, p, rows((m * half + k) * MAIN, MAIN), cols],
                        back_ss.at[t], back_rs.at[t, h], at(c + 2 * m, 2 * to_k + to_p),
                    )

        def return_rest():
            for g, cols in parts:
                wait(back_x.at[t, :, cols], backx_rs.at[t, g])
                back_y[t, :, cols] = dot(shuffle(1), back_x[t, :, cols]).astype(BF16)
                for h in range(nh):
                    to_k = (k + c + 2 * h) % half
                    for flip, to_p in enumerate(parities):
                        self_or_send(
                            h == 0 and flip == 0,
                            back_y.at[t, rows((2 * h + to_p) * yblk, yblk), cols],
                            ret.at[t, p, n_main + h * yblk : n_main + (h + 1) * yblk, cols],
                            backy_ss.at[t], back_rs.at[t, g], at(0, 2 * to_k + to_p),
                        )

        n_chunk = len(chunks)
        for n in range(n_chunk + 3):
            if n == fwd_slot:
                forward_rest()
            if n == chunk_of[None] + 2:
                send_rest()
            if 0 <= n - 1 < n_chunk:
                stage_c(n - 1)
            if n == chunk_of[None] + 2:
                return_rest()
            if 0 <= n - 2 < n_chunk:
                stage_e(n - 2)
            if n < n_chunk:
                stage_a(n)

        for h, cols in parts:
            wait(ret.at[t, :, :, cols], back_rs.at[t, h])
            for q in range(2):
                mix_s[t, q, :, cols] = dot(bm[t, other, :], ret[t, q, :, cols]).astype(BF16)
            send(mix_s.at[t, :, :, cols], mix_r.at[t, :, :, cols], mix_ss.at[t, h], mix_rs.at[t, h], sibling)
            mixed = [
                state[t, :, q * wide + cols.start : q * wide + cols.stop].astype(F32)
                + dot(bm[t, own, :], ret[t, q, :, cols])
                for q in range(2)
            ]
            wait(mix_r.at[t, :, :, cols], mix_rs.at[t, h])
            for q in range(2):
                new[t, q, :, cols] = (mixed[q] + mix_r[t, q, :, cols].astype(F32)).astype(BF16)

            @pl.when(t == 0)
            def _():
                send(new.at[0, :, :, cols], hand.at[:, :, cols], hand_ss.at[h], hand_rs.at[h], ahead)

        @pl.when(t == 0)
        def _():
            for h, cols in parts:
                wait(hand.at[:, :, cols], hand_rs.at[h])
                for q in range(2):
                    part_of = slice(q * wide + cols.start, q * wide + cols.stop)
                    state[1, :, part_of] = jnp.where(s == 0, inc[:, part_of], hand[q, :, cols])
            normalise(1)

        return carry

    lax.fori_loop(0, TICKS, tick, 0)
    for q in range(2):
        out_ref[0, :, q * wide : (q + 1) * wide] = new[1, q]

    for h, cols in parts:
        wait(hand.at[:, :, cols], hand_ss.at[h])
    wait(wmeta.at[:, own, :], meta_ss)
    wait(win.at[slice_own, :], w_ss.at[0])
    wait(wdn.at[slice_own, :], w_ss.at[1])

    def drain(t, carry):
        def sent(ref, block, count, sem):
            @pl.when(c == 0)
            def _():
                wait(ref.at[t, 0 : block * count, :], sem.at[t])

            @pl.when(c == 1)
            def _():
                wait(ref.at[t, 0 : block * (count + 1), :], sem.at[t])

        wait(normed.at[t, own, :], norm_ss.at[t])
        sent(recv, MAIN, 2 * nm * half - 1, main_ss)
        sent(yrest, yblk, 2 * nh - 1, yrest_ss)
        wait(xrest.at[t, 0 : (nx - 1) * xblk, :], xrest_ss.at[t])
        for i in range(len(chunks)):
            a, n = first[i], size[i]
            wait(y_in.at[t, a // 2 : (a + n) // 2, :], y_ss.at[t, i])
            wait(act.at[t, a // 2 : (a + n) // 2, :], acty_ss.at[t, i])
        sent(recv, MAIN, 2 * nm * half - 1, back_ss)
        for h, cols in parts:
            wait(back_x.at[t, 0 : (nx - 1) * xblk, cols], backx_ss.at[t, h])
            wait(mix_s.at[t, :, :, cols], mix_ss.at[t, h])
        sent(yrest, yblk, 2 * nh - 1, backy_ss)
        return carry

    lax.fori_loop(0, TICKS, drain, 0)


def body(section_inputs, incoming, norm_gain, in_weights, down_weights, expert_ids, route_weights):
    ns, count = lax.axis_size("section"), lax.axis_size("expert")
    nx = NX
    ny = count // (2 * nx)
    half = ny // 2
    tok = section_inputs.shape[1]
    ds, ff = in_weights.shape[1], down_weights.shape[2]
    groups = [None] + sorted(range(half), key=lambda d: (-min(d, half - d), d))
    chunks = [2, 3] if half == 4 else [2, 1]
    fwd_slot = 0
    cuts = [ds * 4 // 5, ds * 8 // 5, 2 * ds]
    piece = 32
    dims = (ns, nx, ny, tok, ds, ff, groups, chunks, fwd_slot, cuts, piece)
    both, wide = 2 * tok, 2 * ds
    nm, nh = nx // 2, half // 2
    n_main, n_rest = nm * half * MAIN, nh * nx * REST
    n_rows = n_main + n_rest
    rest_rows = nx * half * REST
    work = half * 2 * nm * MAIN + rest_rows

    def vmem(*shape, dtype=BF16):
        return pltpu.VMEM(shape, dtype)

    def dma(*shape):
        return pltpu.SemaphoreType.DMA(shape) if shape else pltpu.SemaphoreType.DMA

    n, h = len(chunks), len(cuts)
    scratch = [
        vmem(2, tok, 2 * wide), vmem(tok, 2 * wide), vmem(1, 2 * wide, dtype=F32),
        vmem(wide, 2 * ff), vmem(wide, ff), vmem(2, both, 128, dtype=F32),
        vmem(2, n_rows, both), vmem(2, both, n_rows), vmem(2, both, 2 * wide),
        vmem(2, 2, n_main, wide), vmem(2, 2, n_rest, wide), vmem(2, work, wide),
        vmem(2, rest_rows, wide), vmem(2, rest_rows, wide),
        vmem(2, work, 2 * ff), vmem(2, work // 2, 2 * ff), vmem(2, work, ff), vmem(2, work, wide),
        vmem(2, rest_rows, wide), vmem(2, rest_rows, wide), vmem(2, 2, n_rows, wide),
        vmem(2, 2, tok, wide), vmem(2, 2, tok, wide), vmem(2, 2, tok, wide), vmem(2, tok, wide),
        dma(5), dma(2), dma(2), dma(), dma(), dma(2), dma(2), dma(2), dma(2, n),
        dma(2), dma(2), dma(2), dma(2, n), dma(2, n, work // piece), dma(2, n), dma(2, n),
        dma(2), dma(2, h), dma(2, h), dma(2), dma(2, h), dma(2, h), dma(2, h), dma(h), dma(h),
    ]
    in_vmem = pl.BlockSpec(memory_space=pltpu.VMEM)
    anywhere = pl.BlockSpec(memory_space=pl.ANY)
    return pl.pallas_call(
        functools.partial(kernel, dims),
        out_shape=jax.ShapeDtypeStruct(section_inputs.shape, section_inputs.dtype),
        in_specs=[anywhere] * 5 + [in_vmem] * 2,
        out_specs=in_vmem,
        scratch_shapes=scratch,
        compiler_params=pltpu.CompilerParams(
            collective_id=0, has_side_effects=True, vmem_limit_bytes=60 * 1024 * 1024
        ),
        cost_estimate=pl.CostEstimate(
            flops=2 * 2 * work * wide * 3 * ff, bytes_accessed=2 * ds * 3 * ff, transcendentals=work * ff
        ),
        name="relay",
    )(
        section_inputs, incoming, norm_gain, in_weights, down_weights,
        jnp.swapaxes(expert_ids, 2, 3), jnp.swapaxes(route_weights, 2, 3),
    )


def solution(mesh):
    placed = (
        P("section", "expert", None),
        P(None, "expert", None),
        P("section", None),
        P("section", "expert", None),
        P("section", "expert", None),
        P(None, "section", "expert", None),
        P(None, "section", "expert", None),
    )
    return jax.shard_map(
        body, mesh=mesh, in_specs=placed, out_specs=P("section", "expert", None), check_vma=False
    )
```
